32 devices in a mesh: gx: 8 (over y, x, core), gy: 4 (over z).
Axes of the slice: x: 2, y: 2, z: 4, core: 2. Of those that a mesh axis runs over, the one named last changes fastest.
Arguments:
- points_rhs: float32 [16, 524288], P(None, ('gx', 'gy')), may hold values from -6 to 6
- morton_order: int32 [524288], P(('gx', 'gy')), may hold values from 0 to 16383, as said below
- band_offsets: int32 [2048], P(('gx', 'gy')), may hold values from -16 to 16, as said below
- leaf_basis: bfloat16 [2048, 32, 256], P(('gx', 'gy')), may hold values from -0.375 to 0.375
- band_blocks: bfloat16 [2048, 2, 256, 256], P(('gx', 'gy')), may hold values from -0.375 to 0.375
- translations: float32 [32, 5, 8, 2, 32, 32], P(('gx', 'gy'))
- out_basis: bfloat16 [2048, 32, 256], P(('gx', 'gy')), may hold values from -1 to 1
Outputs:
- transformed: float32 [16, 524288], P(None, ('gx', 'gy'))
The draws below stay inside these ranges and needn't reach their ends.
Inputs may be any that keep to these rules, and one draw needn't show every extreme that they name: `morton_order`: for every node k, entries 16384 * k to 16384 * (k + 1) - 1 hold each of 0 to 16383 exactly once. `band_offsets`: never zero; the first leaf of every node has offset -16 and the last leaf of every node has offset 16.
All inputs are finite; a program needn't handle non-finite values.
Results may differ from the reference program's by a relative error of at most 0.0033.
Values may be sent and summed in bfloat16 or wider, within the bound.
A program may use at most 128 MiB of HBM per device.

```python
import math
import jax
import jax.numpy as jnp
from jax import lax

R = 32
LEAF = 256
NRHS = 16
GROUPS = 8
LEAVES_DEV = 64
HW = 16
LEVELS = 5
NODES = 32
PTS_DEV = 16384
LEAVES = 2048
NPTS = 524288


def shuffle_node(node_key):
    return jax.random.permutation(node_key, PTS_DEV)


def draw_morton_order(key, part):
    node_keys = jax.random.split(key, NODES)
    shuffled = jax.vmap(shuffle_node)(node_keys).astype(jnp.int32)
    return shuffled.reshape(NODES * PTS_DEV).astype(jnp.int32)


def draw_band_offsets(key, part):
    key_size, key_sign = jax.random.split(jax.random.fold_in(key, 7), 2)
    magnitude = jax.random.randint(key_size, (LEAVES,), 1, HW + 1).astype(jnp.int32)
    sign = (jax.random.randint(key_sign, (LEAVES,), 0, 2) * 2 - 1).astype(jnp.int32)
    drawn = (magnitude * sign).astype(jnp.int32)
    position = jnp.arange(LEAVES, dtype=jnp.int32) % LEAVES_DEV
    lowest = jnp.full((LEAVES,), -HW, dtype=jnp.int32)
    highest = jnp.full((LEAVES,), HW, dtype=jnp.int32)
    drawn = jnp.where(position == 0, lowest, drawn)
    drawn = jnp.where(position == LEAVES_DEV - 1, highest, drawn)
    return drawn.astype(jnp.int32)


def draw_translations(key, part):
    key_noise, key_diag = jax.random.split(key, 2)
    full_shape = (NODES, LEVELS, GROUPS, 2, R, R)
    jitter = jax.random.normal(key_noise, full_shape, jnp.float32)
    diagonal = jax.random.uniform(key_diag, (NODES, LEVELS, GROUPS, 1, R, 1), jnp.float32, 0.55, 0.85)
    identity = jnp.eye(R, dtype=jnp.float32)
    self_mask = (jnp.arange(2) == 0).astype(jnp.float32).reshape(1, 1, 1, 2, 1, 1)
    spread = (0.15 * self_mask + 0.7 * (1.0 - self_mask)) / math.sqrt(R)
    return (jitter * spread + self_mask * diagonal * identity).astype(jnp.float32)


def block_scale(stream_key, dims, pieces, smallest, top_value):
    level = 1.0
    for dim, blocks in pieces:
        steps = jax.random.uniform(jax.random.fold_in(jax.random.fold_in(stream_key, 6), dim), (blocks,), jnp.float32, smallest / len(pieces), top_value / len(pieces))
        level = level * jnp.repeat(jnp.exp(steps), dims[dim] // blocks).reshape((-1,) + (1,) * (len(dims) - 1 - dim))
    return level


def scatter_about(stream_key, shape, scale, limit, shards=(), held_as=jnp.bfloat16):
    values = jax.random.normal(stream_key, shape, jnp.float32) * scale
    if len(shards) > 0:
        values = block_scale(stream_key, shape, shards, -0.22, 0.18) * values
    return jnp.clip(values, min=-limit, max=limit).astype(held_as)


def setup_inputs(seed: int = 0) -> dict:
    key_list = jax.random.split(jax.random.key(seed), 8)
    return {
        "points_rhs": scatter_about(key_list[0], (NRHS, NPTS), 1.0, 6.0, ((1, 32),), jnp.float32),
        "morton_order": draw_morton_order(jax.random.fold_in(key_list[7], 71), 0),
        "band_offsets": draw_band_offsets(jax.random.fold_in(key_list[7], 71), 0),
        "leaf_basis": scatter_about(key_list[3], (LEAVES, R, LEAF), LEAF ** -0.5, 0.375, ((0, 32),)),
        "band_blocks": scatter_about(key_list[4], (LEAVES, 2, LEAF, LEAF), LEAF ** -0.5, 0.375, ((0, 32),)),
        "translations": draw_translations(jax.random.fold_in(key_list[7], 71), 0),
        "out_basis": scatter_about(key_list[6], (LEAVES, R, LEAF), R ** -0.5, 1.0, ((0, 32),)),
    }


def node_near(node_pair):
    bands, own_block, partner_block = node_pair
    bands_f = bands.astype(jnp.float32)
    own_term = jnp.einsum('lpq,slq->slp', bands_f[:, 0], own_block.astype(jnp.float32), precision=lax.Precision.HIGHEST)
    partner_term = jnp.einsum('lpq,slq->slp', bands_f[:, 1], partner_block.astype(jnp.float32), precision=lax.Precision.HIGHEST)
    return own_term + partner_term


def reference(points_rhs, morton_order, band_offsets, leaf_basis, band_blocks, translations, out_basis):
    node_start = (jnp.arange(NODES, dtype=jnp.int32) * PTS_DEV)[:, None]
    global_order = (morton_order.astype(jnp.int32).reshape(NODES, PTS_DEV) + node_start).reshape(NPTS)
    ordered = points_rhs[:, global_order].astype(jnp.bfloat16)
    leaves = ordered.reshape(NRHS, LEAVES, LEAF).astype(jnp.float32)
    coeffs = jnp.einsum('lrp,slp->lrs', leaf_basis.astype(jnp.float32), leaves, precision=lax.Precision.HIGHEST)
    width = LEAVES_DEV * NRHS
    group_cols = width // GROUPS
    coeffs = coeffs.reshape(NODES, LEAVES_DEV, R, NRHS).transpose(0, 2, 1, 3).reshape(NODES, R, GROUPS, group_cols)
    for level in range(LEVELS):
        stride = 2 ** level
        paired = coeffs.reshape(NODES // (2 * stride), 2, stride, R, GROUPS, group_cols)
        partner = paired[:, ::-1].reshape(NODES, R, GROUPS, group_cols)
        coeffs = jnp.einsum('dgab,dbgm->dagm', translations[:, level, :, 0], coeffs, precision=lax.Precision.HIGHEST) + jnp.einsum('dgab,dbgm->dagm', translations[:, level, :, 1], partner, precision=lax.Precision.HIGHEST)
    coeff_bf = coeffs.astype(jnp.bfloat16).reshape(NODES, R, LEAVES_DEV, NRHS).transpose(0, 2, 1, 3).reshape(LEAVES, R, NRHS)
    far_term = jnp.einsum('lrp,lrs->slp', out_basis.astype(jnp.float32), coeff_bf.astype(jnp.float32), precision=lax.Precision.HIGHEST).reshape(NRHS, NPTS)
    padded = jnp.pad(ordered, ((0, 0), (HW * LEAF, HW * LEAF))).reshape(NRHS, LEAVES + 2 * HW, LEAF)
    block_index = jnp.arange(LEAVES, dtype=jnp.int32) + HW + band_offsets.astype(jnp.int32)
    picked = jnp.take(padded, block_index, axis=1)
    picked_nodes = picked.reshape(NRHS, NODES, LEAVES_DEV, LEAF).transpose(1, 0, 2, 3)
    own_nodes = ordered.reshape(NRHS, NODES, LEAVES_DEV, LEAF).transpose(1, 0, 2, 3)
    blocks_nodes = band_blocks.reshape(NODES, LEAVES_DEV, 2, LEAF, LEAF)
    near_nodes = lax.map(node_near, (blocks_nodes, own_nodes, picked_nodes))
    near_term = near_nodes.transpose(1, 0, 2, 3).reshape(NRHS, NPTS)
    return far_term + near_term
```

```python
import functools

import jax
import jax.numpy as jnp
from jax import lax
from jax.experimental import pallas as pl
from jax.experimental.pallas import tpu as pltpu
from jax.sharding import PartitionSpec as P

HW = 16
BF = jnp.bfloat16
F32 = jnp.float32
MESH = pl.DeviceIdType.MESH
PAIR_BASE = (0, 6, 2, 4)
UNROLL = 4


def kernel(
    nx, ny, levels, low_bits,
    offs, pts_h, order_h, lb_h, band_h, tr_h, ob_h, out_h,
    pts, order, xs, ordx, lb, ob, band, tr, tcat, co, snd, rcv, out,
    load_sem, band_sem, out_sem, halo_s, halo_r, lev_s, lev_r,
):
    gx, gy = lax.axis_index("gx"), lax.axis_index("gy")
    me = gx * ny + gy
    last = nx * ny - 1
    rhs = pts.shape[0]
    leaf = xs.shape[1]
    leaves = order.shape[0]
    low_n = xs.shape[0] // rhs
    groups = co.shape[0]
    per = leaves // groups
    rank = co.shape[1]
    width = co.shape[2]
    after0 = HW + leaves

    loads = [
        pltpu.make_async_copy(pts_h, pts, load_sem.at[0]),
        pltpu.make_async_copy(order_h, order, load_sem.at[1]),
        pltpu.make_async_copy(lb_h, lb, load_sem.at[2]),
        pltpu.make_async_copy(tr_h.at[0], tr, load_sem.at[3]),
        pltpu.make_async_copy(ob_h, ob, load_sem.at[4]),
    ]
    quarter = leaves // 4
    band_loads = [
        pltpu.make_async_copy(
            band_h.at[pl.ds(i * quarter, quarter)], band.at[pl.ds(i * quarter, quarter)], band_sem.at[i]
        )
        for i in range(4)
    ]
    for c in loads + band_loads:
        c.start()

    def partner(k):
        if k < low_bits:
            b = 1 << k
            return gx, gy + b - 2 * b * ((gy // b) % 2)
        b = 1 << (k - low_bits)
        return gx + b - 2 * b * ((gx // b) % 2), gy

    low_id = ((me + last) % (last + 1) // ny, (me + last) % (last + 1) % ny)
    high_id = ((me + 1) % (last + 1) // ny, (me + 1) % (last + 1) % ny)
    barrier = pltpu.get_barrier_semaphore()
    for k in range(levels):
        pl.semaphore_signal(barrier, inc=1, device_id=partner(k), device_id_type=MESH)

    @pl.when(me > 0)
    def _():
        pl.semaphore_signal(barrier, inc=1, device_id=low_id, device_id_type=MESH)

    @pl.when(me < last)
    def _():
        pl.semaphore_signal(barrier, inc=1, device_id=high_id, device_id_type=MESH)

    @pl.when(me == 0)
    def _():
        ordx[pl.ds(0, HW)] = jnp.zeros((HW, rhs, leaf), BF)

    @pl.when(me == last)
    def _():
        ordx[pl.ds(after0, HW)] = jnp.zeros((HW, rhs, leaf), BF)

    loads[0].wait()
    for t in range(low_n):
        xs[t * rhs : (t + 1) * rhs, :] = pts[:, t * leaf : (t + 1) * leaf].astype(BF)
    loads[1].wait()

    key_iota = lax.broadcasted_iota(jnp.int32, (leaf, leaf), 0)
    bits = leaf.bit_length() - 1
    lane_leaf = lax.broadcasted_iota(jnp.int32, (rank, width), 1) // rhs

    def gather_leaf(l):
        o = order[pl.ds(l, 1), :]
        onehot = jnp.where(key_iota == (o & (leaf - 1)), 1.0, 0.0).astype(BF)
        high = jnp.broadcast_to(o >> bits, (rhs, leaf))
        full = jnp.dot(xs[...], onehot, preferred_element_type=F32)
        v = [full[t * rhs : (t + 1) * rhs] for t in range(low_n)]
        b = 0
        while len(v) > 1:
            m = ((high >> b) & 1) == 1
            v = [jnp.where(m, v[2 * i + 1], v[2 * i]) for i in range(len(v) // 2)]
            b += 1
        return v[0].astype(BF)

    def gather_pair(q):
        base = PAIR_BASE[q]

        def body(i, _):
            rows = [gather_leaf(base * per + i * UNROLL + u) for u in range(UNROLL)]
            for u in range(UNROLL):
                ordx[HW + base * per + i * UNROLL + u] = rows[u]
            return 0

        lax.fori_loop(0, 2 * per // UNROLL, body, 0)
        if q == 0:
            loads[2].wait()
        for i in range(2):
            g, pos = base + i, 2 * q + i
            f = lax.dot_general(
                lb[g * per * rank : (g + 1) * per * rank, :],
                ordx[HW + g * per : HW + (g + 1) * per].reshape(width, leaf),
                (((1,), (1,)), ((), ())),
                preferred_element_type=F32,
            )
            c = f[:rank]
            for j in range(1, per):
                c = jnp.where(lane_leaf == j, f[j * rank : (j + 1) * rank], c)
            co[pos] = c
            snd[0, pos] = c.astype(BF)

    half = groups // 2

    def level_copy(k, h):
        return pltpu.make_async_remote_copy(
            src_ref=snd.at[k, pl.ds(h * half, half)],
            dst_ref=rcv.at[k, pl.ds(h * half, half)],
            send_sem=lev_s.at[k, h],
            recv_sem=lev_r.at[k, h],
            device_id=partner(k),
            device_id_type=MESH,
        )

    def translate(k, h):
        level_copy(k, h).wait_recv()
        for p in range(half):
            pos = h * half + p
            g = PAIR_BASE[pos // 2] + pos % 2
            c = co[pos]
            ch = c.astype(BF)
            cl = (c - ch.astype(F32)).astype(BF)
            other = rcv[k, pos]
            stacked = jnp.concatenate([ch, cl, ch, other, other], axis=0)
            new = jnp.dot(tcat[k, g], stacked, preferred_element_type=F32)
            co[pos] = new
            if k + 1 < levels:
                snd[k + 1, pos] = new.astype(BF)
        if k + 1 < levels:
            level_copy(k + 1, h).start()

    down = pltpu.make_async_remote_copy(
        src_ref=ordx.at[pl.ds(HW, HW)],
        dst_ref=ordx.at[pl.ds(after0, HW)],
        send_sem=halo_s.at[0],
        recv_sem=halo_r.at[0],
        device_id=low_id,
        device_id_type=MESH,
    )
    up = pltpu.make_async_remote_copy(
        src_ref=ordx.at[pl.ds(after0 - HW, HW)],
        dst_ref=ordx.at[pl.ds(0, HW)],
        send_sem=halo_s.at[1],
        recv_sem=halo_r.at[1],
        device_id=high_id,
        device_id_type=MESH,
    )

    gather_pair(0)
    has_low, has_high = (me + last - 1) // last, (2 * last - me - 1) // last
    pl.semaphore_wait(barrier, levels + has_low + has_high)

    @pl.when(me > 0)
    def _():
        down.start()

    gather_pair(1)
    level_copy(0, 0).start()

    @pl.when(me < last)
    def _():
        up.start()

    loads[3].wait()

    def cat_body(i, _):
        k, g = i // groups, i % groups
        t0, t1 = tr[k, g, 0], tr[k, g, 1]
        h0, h1 = t0.astype(BF).astype(F32), t1.astype(BF).astype(F32)
        tcat[k, g] = jnp.concatenate([h0, h0, t0 - h0, h1, t1 - h1], axis=1).astype(BF)
        return 0

    lax.fori_loop(0, levels * groups, cat_body, 0)
    gather_pair(2)
    translate(0, 0)
    gather_pair(3)
    level_copy(0, 1).start()
    translate(1, 0)

    @pl.when(me < last)
    def _():
        down.wait_recv()

    @pl.when(me > 0)
    def _():
        up.wait_recv()

    def near(seg):
        band_loads[seg].wait()

        def body(i, _):
            l = seg * quarter + i
            own = ordx[l + HW]
            part = ordx[l + HW + offs[l]]
            dims = (((1,), (1,)), ((), ()))
            r = lax.dot_general(own, band[l, 0], dims, preferred_element_type=F32)
            r += lax.dot_general(part, band[l, 1], dims, preferred_element_type=F32)
            out[:, pl.ds(pl.multiple_of(l * leaf, leaf), leaf)] = r
            return 0

        lax.fori_loop(0, quarter, body, 0)

    row_leaf = lax.broadcasted_iota(jnp.int32, (per * rank, width), 0) // rank
    col_leaf = lax.broadcasted_iota(jnp.int32, (per * rank, width), 1) // rhs
    diagonal = row_leaf == col_leaf
    span = per * leaf

    def out_copy(g):
        return pltpu.make_async_copy(
            out.at[:, pl.ds(g * span, span)], out_h.at[:, pl.ds(g * span, span)], out_sem.at[g]
        )

    def far(h):
        for p in range(half):
            pos = h * half + p
            g = PAIR_BASE[pos // 2] + pos % 2
            c = co[pos].astype(BF).astype(F32)
            tiled = jnp.where(diagonal, jnp.concatenate([c] * per, axis=0), 0.0)
            f = lax.dot_general(
                tiled.T.astype(BF),
                ob[g * per * rank : (g + 1) * per * rank, :],
                (((1,), (0,)), ((), ())),
                preferred_element_type=F32,
            )
            for j in range(per):
                at = (g * per + j) * leaf
                out[:, at : at + leaf] = out[:, at : at + leaf] + f[j * rhs : (j + 1) * rhs]
            out_copy(g).start()

    todo = [list(range(2, levels)), list(range(levels))]
    for seg in range(4):
        near(seg)
        for h in range(2):
            if todo[h]:
                translate(todo[h].pop(0), h)
    loads[4].wait()
    while todo[0]:
        for h in range(2):
            if todo[h]:
                translate(todo[h].pop(0), h)
    far(0)
    while todo[1]:
        translate(todo[1].pop(0), 1)
    far(1)

    for k in range(levels):
        for h in range(2):
            level_copy(k, h).wait_send()

    @pl.when(me > 0)
    def _():
        down.wait_send()

    @pl.when(me < last)
    def _():
        up.wait_send()

    for g in range(groups):
        out_copy(g).wait()


def solution(mesh):
    nx, ny = mesh.shape["gx"], mesh.shape["gy"]
    low_bits = ny.bit_length() - 1

    def local(points_rhs, morton_order, band_offsets, leaf_basis, band_blocks, translations, out_basis):
        rhs, points = points_rhs.shape
        leaves, rank, leaf = leaf_basis.shape
        levels, groups = translations.shape[1:3]
        width = leaves // groups * rhs
        anywhere = pl.BlockSpec(memory_space=pl.ANY)
        dma = pltpu.SemaphoreType.DMA
        return pl.pallas_call(
            functools.partial(kernel, nx, ny, levels, low_bits),
            out_shape=jax.ShapeDtypeStruct((rhs, points), F32),
            in_specs=[pl.BlockSpec(memory_space=pltpu.SMEM)] + [anywhere] * 6,
            out_specs=anywhere,
            scratch_shapes=[
                pltpu.VMEM((rhs, points), F32),
                pltpu.VMEM((leaves, leaf), jnp.int32),
                pltpu.VMEM((points // leaf * rhs, leaf), BF),
                pltpu.VMEM((leaves + 2 * HW, rhs, leaf), BF),
                pltpu.VMEM((leaves * rank, leaf), BF),
                pltpu.VMEM((leaves * rank, leaf), BF),
                pltpu.VMEM((leaves, 2, leaf, leaf), BF),
                pltpu.VMEM((levels, groups, 2, rank, rank), F32),
                pltpu.VMEM((levels, groups, rank, 5 * rank), BF),
                pltpu.VMEM((groups, rank, width), F32),
                pltpu.VMEM((levels, groups, rank, width), BF),
                pltpu.VMEM((levels, groups, rank, width), BF),
                pltpu.VMEM((rhs, points), F32),
                dma((5,)),
                dma((4,)),
                dma((groups,)),
                dma((2,)),
                dma((2,)),
                dma((levels, 2)),
                dma((levels, 2)),
            ],
            compiler_params=pltpu.CompilerParams(
                collective_id=0, has_side_effects=True, vmem_limit_bytes=48 * 1024 * 1024
            ),
            cost_estimate=pl.CostEstimate(flops=10**10, bytes_accessed=22 * 10**6, transcendentals=0),
        )(
            band_offsets,
            points_rhs,
            morton_order.reshape(leaves, leaf),
            leaf_basis.reshape(leaves * rank, leaf),
            band_blocks,
            translations,
            out_basis.reshape(leaves * rank, leaf),
        )

    return jax.shard_map(
        local,
        mesh=mesh,
        in_specs=(
            P(None, ("gx", "gy")),
            P(("gx", "gy")),
            P(("gx", "gy")),
            P(("gx", "gy"), None, None),
            P(("gx", "gy"), None, None, None),
            P(("gx", "gy"), None, None, None, None, None),
            P(("gx", "gy"), None, None),
        ),
        out_specs=P(None, ("gx", "gy")),
        check_vma=False,
    )
```

```python
import functools

import jax
import jax.numpy as jnp
from jax import lax
from jax.experimental import pallas as pl
from jax.experimental.pallas import tpu as pltpu
from jax.sharding import PartitionSpec as P

HW = 16
LANES = 128
BF = jnp.bfloat16
F32 = jnp.float32
MESH = pl.DeviceIdType.MESH
PAIR_BASE = (0, 6, 2, 4)
UNROLL = 8
NEAR_BATCH = 1


def kernel(
    nx, ny, levels, low_bits,
    offs, pts_h, order_h, lb_h, band_h, tr_h, ob_h, out_h,
    pts, order, xs, ordx, lb, ob, band, tr, tcat, co, snd, rcv, out,
    load_sem, band_sem, out_sem, halo_s, halo_r, lev_s, lev_r,
):
    gx, gy = lax.axis_index("gx"), lax.axis_index("gy")
    me = gx * ny + gy
    last = nx * ny - 1
    rhs = pts.shape[0]
    leaf = xs.shape[1]
    leaves = band.shape[0]
    low_n = xs.shape[0] // rhs
    groups = co.shape[0]
    per = leaves // groups
    rank = co.shape[1]
    width = co.shape[2]
    after0 = HW + leaves

    loads = [
        pltpu.make_async_copy(pts_h, pts, load_sem.at[0]),
        pltpu.make_async_copy(order_h, order, load_sem.at[1]),
        pltpu.make_async_copy(lb_h, lb, load_sem.at[2]),
        pltpu.make_async_copy(tr_h.at[0], tr, load_sem.at[3]),
        pltpu.make_async_copy(ob_h, ob, load_sem.at[4]),
    ]
    quarter = leaves // 4
    band_loads = [
        pltpu.make_async_copy(
            band_h.at[pl.ds(i * quarter, quarter)], band.at[pl.ds(i * quarter, quarter)], band_sem.at[i]
        )
        for i in range(4)
    ]
    for c in loads + band_loads:
        c.start()

    def partner(k):
        if k < low_bits:
            b = 1 << k
            return gx, gy + b - 2 * b * ((gy // b) % 2)
        b = 1 << (k - low_bits)
        return gx + b - 2 * b * ((gx // b) % 2), gy

    low_id = ((me + last) % (last + 1) // ny, (me + last) % (last + 1) % ny)
    high_id = ((me + 1) % (last + 1) // ny, (me + 1) % (last + 1) % ny)
    barrier = pltpu.get_barrier_semaphore()
    for k in range(levels):
        pl.semaphore_signal(barrier, inc=1, device_id=partner(k), device_id_type=MESH)

    @pl.when(me > 0)
    def _():
        pl.semaphore_signal(barrier, inc=1, device_id=low_id, device_id_type=MESH)

    @pl.when(me < last)
    def _():
        pl.semaphore_signal(barrier, inc=1, device_id=high_id, device_id_type=MESH)

    @pl.when(me == 0)
    def _():
        ordx[pl.ds(0, HW)] = jnp.zeros((HW, rhs, leaf), BF)

    @pl.when(me == last)
    def _():
        ordx[pl.ds(after0, HW)] = jnp.zeros((HW, rhs, leaf), BF)

    loads[0].wait()
    for t in range(low_n):
        xs[t * rhs : (t + 1) * rhs, :] = pts[:, t * leaf : (t + 1) * leaf].astype(BF)
    loads[1].wait()

    key_iota = lax.broadcasted_iota(jnp.int32, (leaf, leaf), 0)
    bits = leaf.bit_length() - 1
    lane_leaf = lax.broadcasted_iota(jnp.int32, (rank, width), 1) // rhs

    def gather_leaf(l):
        parts = order.shape[1]
        o = jnp.concatenate([order[pl.ds(l * (leaf // parts) + i, 1), :] for i in range(leaf // parts)], axis=1)
        onehot = jnp.where(key_iota == (o & (leaf - 1)), 1.0, 0.0).astype(BF)
        high = jnp.broadcast_to(o >> bits, (rhs, leaf))
        full = jnp.dot(xs[...], onehot, preferred_element_type=F32)
        v = [full[t * rhs : (t + 1) * rhs] for t in range(low_n)]
        b = 0
        while len(v) > 1:
            m = ((high >> b) & 1) == 1
            v = [jnp.where(m, v[2 * i + 1], v[2 * i]) for i in range(len(v) // 2)]
            b += 1
        return v[0].astype(BF)

    def gather_pair(q):
        base = PAIR_BASE[q]

        def body(i, _):
            rows = [gather_leaf(base * per + i * UNROLL + u) for u in range(UNROLL)]
            for u in range(UNROLL):
                ordx[HW + base * per + i * UNROLL + u] = rows[u]
            return 0

        lax.fori_loop(0, 2 * per // UNROLL, body, 0)
        if q == 0:
            loads[2].wait()
        for i in range(2):
            g, pos = base + i, 2 * q + i
            f = lax.dot_general(
                lb[g * per * rank : (g + 1) * per * rank, :],
                ordx[HW + g * per : HW + (g + 1) * per].reshape(width, leaf),
                (((1,), (1,)), ((), ())),
                preferred_element_type=F32,
            )
            c = f[:rank]
            for j in range(1, per):
                c = jnp.where(lane_leaf == j, f[j * rank : (j + 1) * rank], c)
            co[pos] = c
            snd[0, pos] = c.astype(BF)

    half = groups // 2

    def level_copy(k, h):
        return pltpu.make_async_remote_copy(
            src_ref=snd.at[k, pl.ds(h * half, half)],
            dst_ref=rcv.at[k, pl.ds(h * half, half)],
            send_sem=lev_s.at[k, h],
            recv_sem=lev_r.at[k, h],
            device_id=partner(k),
            device_id_type=MESH,
        )

    def translate(k, h):
        level_copy(k, h).wait_recv()
        for p in range(half):
            pos = h * half + p
            g = PAIR_BASE[pos // 2] + pos % 2
            c = co[pos]
            ch = c.astype(BF)
            cl = (c - ch.astype(F32)).astype(BF)
            other = rcv[k, pos]
            stacked = jnp.concatenate([ch, cl, ch, other, other], axis=0)
            new = jnp.dot(tcat[k, g], stacked, preferred_element_type=F32)
            co[pos] = new
            if k + 1 < levels:
                snd[k + 1, pos] = new.astype(BF)
        if k + 1 < levels:
            level_copy(k + 1, h).start()

    down = pltpu.make_async_remote_copy(
        src_ref=ordx.at[pl.ds(HW, HW)],
        dst_ref=ordx.at[pl.ds(after0, HW)],
        send_sem=halo_s.at[0],
        recv_sem=halo_r.at[0],
        device_id=low_id,
        device_id_type=MESH,
    )
    up = pltpu.make_async_remote_copy(
        src_ref=ordx.at[pl.ds(after0 - HW, HW)],
        dst_ref=ordx.at[pl.ds(0, HW)],
        send_sem=halo_s.at[1],
        recv_sem=halo_r.at[1],
        device_id=high_id,
        device_id_type=MESH,
    )

    gather_pair(0)
    has_low, has_high = (me + last - 1) // last, (2 * last - me - 1) // last
    pl.semaphore_wait(barrier, levels + has_low + has_high)

    @pl.when(me > 0)
    def _():
        down.start()

    gather_pair(1)
    level_copy(0, 0).start()

    @pl.when(me < last)
    def _():
        up.start()

    loads[3].wait()

    def cat_body(k, _):
        for g in range(groups):
            t0, t1 = tr[k, g, 0], tr[k, g, 1]
            h0, h1 = t0.astype(BF).astype(F32), t1.astype(BF).astype(F32)
            tcat[k, g] = jnp.concatenate([h0, h0, t0 - h0, h1, t1 - h1], axis=1).astype(BF)
        return 0

    lax.fori_loop(0, levels, cat_body, 0)
    gather_pair(2)
    translate(0, 0)
    gather_pair(3)
    level_copy(0, 1).start()
    translate(1, 0)

    @pl.when(me < last)
    def _():
        down.wait_recv()

    @pl.when(me > 0)
    def _():
        up.wait_recv()

    leaf_lane = lax.broadcasted_iota(jnp.int32, (leaf, width), 1) // rhs

    def near(seg):
        band_loads[seg].wait()

        for g in range(seg * groups // 4, (seg + 1) * groups // 4):
            own = ordx[HW + g * per : HW + (g + 1) * per].reshape(width, leaf)
            picked = [ordx[l + HW + offs[l]] for l in range(g * per, (g + 1) * per)]
            part = jnp.concatenate(picked, axis=0)
            dims = (((1,), (1,)), ((), ()))
            total = None
            for j in range(0, per, NEAR_BATCH):
                at = pl.ds(g * per + j, NEAR_BATCH)
                flat = (NEAR_BATCH * leaf, leaf)
                f = lax.dot_general(band[at, 0].reshape(flat), own, dims, preferred_element_type=F32)
                f += lax.dot_general(band[at, 1].reshape(flat), part, dims, preferred_element_type=F32)
                for i in range(NEAR_BATCH):
                    piece = f[i * leaf : (i + 1) * leaf]
                    total = piece if total is None else jnp.where(leaf_lane == j + i, piece, total)
            total = total.T
            for j in range(per):
                at = (g * per + j) * leaf
                out[:, at : at + leaf] = total[j * rhs : (j + 1) * rhs]

    row_leaf = lax.broadcasted_iota(jnp.int32, (per * rank, width), 0) // rank
    col_leaf = lax.broadcasted_iota(jnp.int32, (per * rank, width), 1) // rhs
    diagonal = row_leaf == col_leaf
    span = per * leaf

    def out_copy(g):
        return pltpu.make_async_copy(
            out.at[:, pl.ds(g * span, span)], out_h.at[:, pl.ds(g * span, span)], out_sem.at[g]
        )

    def far(h):
        for p in range(half):
            pos = h * half + p
            g = PAIR_BASE[pos // 2] + pos % 2
            c = co[pos].astype(BF).astype(F32)
            tiled = jnp.where(diagonal, jnp.concatenate([c] * per, axis=0), 0.0)
            f = lax.dot_general(
                tiled.T.astype(BF),
                ob[g * per * rank : (g + 1) * per * rank, :],
                (((1,), (0,)), ((), ())),
                preferred_element_type=F32,
            )
            for j in range(per):
                at = (g * per + j) * leaf
                out[:, at : at + leaf] = out[:, at : at + leaf] + f[j * rhs : (j + 1) * rhs]
            out_copy(g).start()

    todo = [list(range(2, levels)), list(range(levels))]
    for seg in range(4):
        near(seg)
        for h in range(2):
            if todo[h]:
                translate(todo[h].pop(0), h)
    loads[4].wait()
    while todo[0]:
        for h in range(2):
            if todo[h]:
                translate(todo[h].pop(0), h)
    far(0)
    while todo[1]:
        translate(todo[1].pop(0), 1)
    far(1)

    for k in range(levels):
        for h in range(2):
            level_copy(k, h).wait_send()

    @pl.when(me > 0)
    def _():
        down.wait_send()

    @pl.when(me < last)
    def _():
        up.wait_send()

    for g in range(groups):
        out_copy(g).wait()


def solution(mesh):
    nx, ny = mesh.shape["gx"], mesh.shape["gy"]
    low_bits = ny.bit_length() - 1

    def local(points_rhs, morton_order, band_offsets, leaf_basis, band_blocks, translations, out_basis):
        rhs, points = points_rhs.shape
        leaves, rank, leaf = leaf_basis.shape
        levels, groups = translations.shape[1:3]
        width = leaves // groups * rhs
        anywhere = pl.BlockSpec(memory_space=pl.ANY)
        dma = pltpu.SemaphoreType.DMA
        return pl.pallas_call(
            functools.partial(kernel, nx, ny, levels, low_bits),
            out_shape=jax.ShapeDtypeStruct((rhs, points), F32),
            in_specs=[pl.BlockSpec(memory_space=pltpu.SMEM)] + [anywhere] * 6,
            out_specs=anywhere,
            scratch_shapes=[
                pltpu.VMEM((rhs, points), F32),
                pltpu.VMEM((points // LANES, LANES), jnp.int32),
                pltpu.VMEM((points // leaf * rhs, leaf), BF),
                pltpu.VMEM((leaves + 2 * HW, rhs, leaf), BF),
                pltpu.VMEM((leaves * rank, leaf), BF),
                pltpu.VMEM((leaves * rank, leaf), BF),
                pltpu.VMEM((leaves, 2, leaf, leaf), BF),
                pltpu.VMEM((levels, groups, 2, rank, rank), F32),
                pltpu.VMEM((levels, groups, rank, 5 * rank), BF),
                pltpu.VMEM((groups, rank, width), F32),
                pltpu.VMEM((levels, groups, rank, width), BF),
                pltpu.VMEM((levels, groups, rank, width), BF),
                pltpu.VMEM((rhs, points), F32),
                dma((5,)),
                dma((4,)),
                dma((groups,)),
                dma((2,)),
                dma((2,)),
                dma((levels, 2)),
                dma((levels, 2)),
            ],
            compiler_params=pltpu.CompilerParams(
                collective_id=0, has_side_effects=True, vmem_limit_bytes=60 * 1024 * 1024
            ),
            cost_estimate=pl.CostEstimate(flops=10**10, bytes_accessed=22 * 10**6, transcendentals=0),
        )(
            band_offsets,
            points_rhs,
            morton_order.reshape(points // LANES, LANES),
            leaf_basis.reshape(leaves * rank, leaf),
            band_blocks,
            translations,
            out_basis.reshape(leaves * rank, leaf),
        )

    return jax.shard_map(
        local,
        mesh=mesh,
        in_specs=(
            P(None, ("gx", "gy")),
            P(("gx", "gy")),
            P(("gx", "gy")),
            P(("gx", "gy"), None, None),
            P(("gx", "gy"), None, None, None),
            P(("gx", "gy"), None, None, None, None, None),
            P(("gx", "gy"), None, None),
        ),
        out_specs=P(None, ("gx", "gy")),
        check_vma=False,
    )
```
